32 devices in a mesh: dp: 8 (over z, x), tensor: 4 (over y, core).
Axes of the slice: x: 2, y: 2, z: 4, core: 2. Of those that a mesh axis runs over, the one named last changes fastest.
Arguments:
- tokens: bfloat16 [1024, 9216], P(('dp', 'tensor')), may hold values from -6 to 6
- gain: bfloat16 [9216], replicated, may hold values from 0.25 to 1.75
- up_weight: bfloat16 [2304, 9216], P('tensor', 'dp'), may hold values from -0.0625 to 0.0625
- down_weight: bfloat16 [2304, 9216], P('tensor', 'dp'), may hold values from -0.125 to 0.125
- grad_out: bfloat16 [1024, 9216], P(('dp', 'tensor')), may hold values from -6 to 6
Outputs:
- grad_tokens: bfloat16 [1024, 9216], P(('dp', 'tensor'))
- grad_gain: float32 [9216], replicated
- grad_up: bfloat16 [2304, 9216], P('tensor', 'dp')
- grad_down: bfloat16 [2304, 9216], P('tensor', 'dp')
The draws below stay inside these ranges and needn't reach their ends.
All inputs are finite; a program needn't handle non-finite values.
Results may differ from the reference program's by a relative error of at most 0.012.
Values may be sent and summed in bfloat16 or wider, within the bound.
A program may use at most 128 MiB of HBM per device.

```python
import jax
import jax.numpy as jnp
from jax import lax

D = 9216
FF = 2304
TOK_DEV = 32
TOKENS = 1024
N_DP = 8
N_TENSOR = 4


def levels(stream_key, extent, split, low, top_value):
    def one(position, shards_of):
        draws = jax.random.uniform(jax.random.fold_in(jax.random.fold_in(stream_key, 6), position), (shards_of,), jnp.float32, low / len(split), top_value / len(split))
        return jnp.repeat(jnp.exp(draws), extent[position] // shards_of).reshape((-1,) + (1,) * (len(extent) - position - 1))

    factor_of = one(*split[0])
    for cut in split[1:]:
        factor_of = factor_of * one(*cut)
    return factor_of


def normal_values(own_key, dims, width, bound, pieces=(), kind=jnp.bfloat16):
    level = levels(own_key, dims, pieces, -0.22, 0.18) if pieces else 1.0
    drawn = jax.random.normal(own_key, dims, jnp.float32) * width * level
    return jnp.minimum(jnp.maximum(drawn, -bound), bound).astype(kind)


def setup_inputs(seed: int = 0) -> dict:
    key_of = jax.random.split(jax.random.key(seed), 6)
    return {
        "tokens": normal_values(key_of[0], (TOKENS, D), 1.0, 6.0, ((0, 32),)),
        "gain": jnp.clip(1.0 + 0.15 * jax.random.normal(key_of[1], (D,), jnp.float32), 0.25, 1.75).astype(jnp.bfloat16),
        "up_weight": normal_values(key_of[2], (FF, D), D ** -0.5, 0.0625, ((0, 4), (1, 8))),
        "down_weight": normal_values(key_of[3], (FF, D), FF ** -0.5, 0.125, ((0, 4), (1, 8))),
        "grad_out": normal_values(key_of[4], (TOKENS, D), 1.0, 6.0, ((0, 32),)),
    }


epsilon = 1e-05

def rounded(value):
    return lax.optimization_barrier(value.astype(jnp.bfloat16)).astype(jnp.float32)

def reference(tokens, gain, up_weight, down_weight, grad_out):
    floated = tokens.astype(jnp.float32)
    inv_rms = lax.rsqrt(lax.optimization_barrier(jnp.mean(floated * floated, axis=-1, keepdims=True)) + epsilon)
    unit_rows = floated * inv_rms
    gain_float = gain.astype(jnp.float32)
    normed = (unit_rows * gain_float).astype(jnp.bfloat16)
    contract_last = (((1,), (1,)), ((), ()))
    pre_act = lax.dot_general(normed, up_weight, contract_last, preferred_element_type=jnp.float32)
    back_act = lax.dot_general(grad_out, down_weight, contract_last, preferred_element_type=jnp.float32)
    lifted = jnp.maximum(pre_act, 0.0)
    hidden_act = (lifted * lifted).astype(jnp.bfloat16)
    grad_pre = (back_act * (2.0 * lifted)).astype(jnp.bfloat16)
    row_group = TOK_DEV * N_TENSOR
    contract_rows = (((0,), (0,)), ((), ()))

    def batch_step(carry, index):
        first = (index * row_group).astype(jnp.int32)
        norm_rows = lax.dynamic_slice_in_dim(normed, first, row_group, 0)
        pre_rows = lax.dynamic_slice_in_dim(grad_pre, first, row_group, 0)
        cot_rows = lax.dynamic_slice_in_dim(grad_out, first, row_group, 0)
        act_rows = lax.dynamic_slice_in_dim(hidden_act, first, row_group, 0)
        up_term = lax.dot_general(pre_rows, norm_rows, contract_rows, preferred_element_type=jnp.float32)
        down_term = lax.dot_general(act_rows, cot_rows, contract_rows, preferred_element_type=jnp.float32)
        return ((carry[0] + rounded(up_term), carry[1] + rounded(down_term)), None)
    start_sums = (jnp.zeros((FF, D), jnp.float32), jnp.zeros((FF, D), jnp.float32))
    sums, unused = lax.scan(batch_step, start_sums, jnp.arange(N_DP, dtype=jnp.int32))
    grad_up = sums[0].astype(jnp.bfloat16)
    grad_down = sums[1].astype(jnp.bfloat16)
    block_cols = FF // N_TENSOR

    def block_step(carry, index):
        first = (index * block_cols).astype(jnp.int32)
        pre_cols = lax.dynamic_slice_in_dim(grad_pre, first, block_cols, 1)
        up_rows = lax.dynamic_slice_in_dim(up_weight, first, block_cols, 0)
        term = jnp.dot(pre_cols, up_rows, preferred_element_type=jnp.float32)
        return (carry + rounded(term), None)
    grad_normed, unused_two = lax.scan(block_step, jnp.zeros((TOKENS, D), jnp.float32), jnp.arange(N_TENSOR, dtype=jnp.int32))
    grad_gain = lax.optimization_barrier(jnp.sum(grad_normed * unit_rows, axis=0))
    grad_unit = grad_normed * gain_float
    mean_term = lax.optimization_barrier(jnp.mean(grad_unit * unit_rows, axis=-1, keepdims=True))
    grad_tokens = (inv_rms * (grad_unit - unit_rows * mean_term)).astype(jnp.bfloat16)
    return (grad_tokens, grad_gain, grad_up, grad_down)
```

```python
import jax
import jax.numpy as jnp
from jax import lax
from jax.sharding import PartitionSpec as P

epsilon = 1e-05


def local(tokens, gain, up_weight, down_weight, grad_out):
    gain_float = gain.astype(jnp.float32)
    floated = tokens.astype(jnp.float32)
    inv_rms = lax.rsqrt(jnp.mean(floated * floated, axis=-1, keepdims=True) + epsilon)
    unit_rows = floated * inv_rms
    normed = (unit_rows * gain_float).astype(jnp.bfloat16)

    def to_columns(rows):
        part = lax.all_to_all(rows, "dp", split_axis=1, concat_axis=0, tiled=True)
        return lax.all_gather(part, "tensor", axis=0, tiled=True)

    grads_cols = to_columns(grad_out)
    normed_cols = to_columns(normed)
    contract_last = (((1,), (1,)), ((), ()))
    back_part = lax.dot_general(
        grads_cols, down_weight, contract_last, preferred_element_type=jnp.float32
    ).astype(jnp.bfloat16)
    pre_part = lax.dot_general(
        normed_cols, up_weight, contract_last, preferred_element_type=jnp.float32
    ).astype(jnp.bfloat16)
    back_act = lax.psum_scatter(back_part, "dp", scatter_dimension=0, tiled=True)
    pre_act = lax.psum_scatter(pre_part, "dp", scatter_dimension=0, tiled=True)
    lifted = jnp.maximum(pre_act.astype(jnp.float32), 0.0)
    hidden_part = (lifted * lifted).astype(jnp.bfloat16)
    grad_pre_part = (back_act.astype(jnp.float32) * (2.0 * lifted)).astype(jnp.bfloat16)
    grad_pre = lax.all_gather(grad_pre_part, "dp", axis=0, tiled=True)
    hidden_act = lax.all_gather(hidden_part, "dp", axis=0, tiled=True)
    grad_normed_part = jnp.dot(
        grad_pre, up_weight, preferred_element_type=jnp.float32
    ).astype(jnp.bfloat16)
    grad_normed = lax.psum_scatter(grad_normed_part, "tensor", scatter_dimension=0, tiled=True)
    grad_normed = lax.all_to_all(
        grad_normed, "dp", split_axis=0, concat_axis=1, tiled=True
    ).astype(jnp.float32)
    contract_rows = (((0,), (0,)), ((), ()))
    grad_up = lax.dot_general(
        grad_pre, normed_cols, contract_rows, preferred_element_type=jnp.float32
    ).astype(jnp.bfloat16)
    grad_down = lax.dot_general(
        hidden_act, grads_cols, contract_rows, preferred_element_type=jnp.float32
    ).astype(jnp.bfloat16)
    grad_gain = lax.psum(jnp.sum(grad_normed * unit_rows, axis=0), ("dp", "tensor"))
    grad_unit = grad_normed * gain_float
    mean_term = jnp.mean(grad_unit * unit_rows, axis=-1, keepdims=True)
    grad_tokens = (inv_rms * (grad_unit - unit_rows * mean_term)).astype(jnp.bfloat16)
    return (grad_tokens, grad_gain, grad_up, grad_down)


def solution(mesh):
    rows = P(("dp", "tensor"), None)
    weights = P("tensor", "dp")
    return jax.shard_map(
        local,
        mesh=mesh,
        in_specs=(rows, P(), weights, weights, rows),
        out_specs=(rows, P(), weights, weights),
        check_vma=False,
    )
```

```python
import functools

import jax
import jax.numpy as jnp
from jax import lax
from jax.experimental import pallas as pl
from jax.experimental.pallas import tpu as pltpu
from jax.sharding import PartitionSpec as P

MESH = pl.DeviceIdType.MESH

epsilon = 1e-05


def local(tokens, gain, up_weight, down_weight, grad_out):
    gain_float = gain.astype(jnp.float32)
    floated = tokens.astype(jnp.float32)
    inv_rms = lax.rsqrt(jnp.mean(floated * floated, axis=-1, keepdims=True) + epsilon)
    unit_rows = floated * inv_rms
    normed = (unit_rows * gain_float).astype(jnp.bfloat16)

    def to_columns(rows):
        part = lax.all_to_all(rows, "dp", split_axis=1, concat_axis=0, tiled=True)
        return lax.all_gather(part, "tensor", axis=0, tiled=True)

    grads_cols = to_columns(grad_out)
    normed_cols = to_columns(normed)
    contract_last = (((1,), (1,)), ((), ()))
    back_part = lax.dot_general(
        grads_cols, down_weight, contract_last, preferred_element_type=jnp.float32
    ).astype(jnp.bfloat16)
    pre_part = lax.dot_general(
        normed_cols, up_weight, contract_last, preferred_element_type=jnp.float32
    ).astype(jnp.bfloat16)
    back_act = lax.psum_scatter(back_part, "dp", scatter_dimension=0, tiled=True)
    pre_act = lax.psum_scatter(pre_part, "dp", scatter_dimension=0, tiled=True)
    lifted = jnp.maximum(pre_act.astype(jnp.float32), 0.0)
    hidden_part = (lifted * lifted).astype(jnp.bfloat16)
    grad_pre_part = (back_act.astype(jnp.float32) * (2.0 * lifted)).astype(jnp.bfloat16)
    grad_pre = lax.all_gather(grad_pre_part, "dp", axis=0, tiled=True)
    hidden_act = lax.all_gather(hidden_part, "dp", axis=0, tiled=True)
    grad_normed_part = jnp.dot(
        grad_pre, up_weight, preferred_element_type=jnp.float32
    ).astype(jnp.bfloat16)
    grad_normed = lax.psum_scatter(grad_normed_part, "tensor", scatter_dimension=0, tiled=True)
    grad_normed = lax.all_to_all(
        grad_normed, "dp", split_axis=0, concat_axis=1, tiled=True
    ).astype(jnp.float32)
    contract_rows = (((0,), (0,)), ((), ()))
    grad_up = lax.dot_general(
        grad_pre, normed_cols, contract_rows, preferred_element_type=jnp.float32
    ).astype(jnp.bfloat16)
    grad_down = lax.dot_general(
        hidden_act, grads_cols, contract_rows, preferred_element_type=jnp.float32
    ).astype(jnp.bfloat16)
    grad_gain = lax.psum(jnp.sum(grad_normed * unit_rows, axis=0), ("dp", "tensor"))
    grad_unit = grad_normed * gain_float
    mean_term = jnp.mean(grad_unit * unit_rows, axis=-1, keepdims=True)
    grad_tokens = (inv_rms * (grad_unit - unit_rows * mean_term)).astype(jnp.bfloat16)
    return (grad_tokens, grad_gain, grad_up, grad_down)


def kernel(
    tokens, gain_row, gain_own, up, down, grad_out,
    out_tokens, out_gain, out_up, out_down,
    inv_rms, normed, ncols, gcols, part, recvx, sumz, recvz, gp, hid,
    esend, ecore, ysend, ey, gnf, gnb, gnrows, gsum, grecv, gshare,
    a2a_s, a2a_r, tens_s, tens_r, x_s, x_r, z_s, z_r, gz_s, gz_r, gx_s, gx_r,
    e_s, e_r, back_s, back_r, gt_s, gt_r, gd_s, gd_r,
):
    n_dp, n_t, n_z = 8, 4, 4
    rows, columns = tokens.shape[0], up.shape[1]
    hidden = up.shape[0]
    block = n_dp * rows
    chunk = n_t * rows
    d, t = lax.axis_index("dp"), lax.axis_index("tensor")
    z, x = d // 2, d % 2
    y, c = t // 2, t % 2
    x_peer = (z * 2 + 1 - x, t)
    y_peer = (d, (1 - y) * 2 + c)
    core_peer = (d, y * 2 + 1 - c)

    def dp_peer(k):
        return (lax.rem(d + k, n_dp), t)

    def z_peer(k):
        return (lax.rem(z + k, n_z) * 2 + x, t)

    def t_peer(k):
        return (d, lax.rem(t + k, n_t))

    def send(src, dst, s, r, to):
        copy = pltpu.make_async_remote_copy(
            src_ref=src, dst_ref=dst, send_sem=s, recv_sem=r, device_id=to, device_id_type=MESH
        )
        copy.start()
        sent.append(copy)

    sent = []

    def arrived(dst, s, r):
        pltpu.make_async_remote_copy(
            src_ref=dst, dst_ref=dst, send_sem=s, recv_sem=r, device_id=x_peer, device_id_type=MESH
        ).wait_recv()

    def cols_of(i):
        return pl.ds(pl.multiple_of(i * columns, 128), columns)

    def rows_of(i, size):
        return pl.ds(pl.multiple_of(i * size, 32), size)

    def lanes_of(i):
        return pl.ds(pl.multiple_of(i * chunk, 128), chunk)

    barrier = pltpu.get_barrier_semaphore()
    for k in range(1, n_dp):
        pl.semaphore_signal(barrier, inc=1, device_id=dp_peer(k), device_id_type=MESH)
    for k in range(1, n_t):
        pl.semaphore_signal(barrier, inc=1, device_id=t_peer(k), device_id_type=MESH)
    pl.semaphore_wait(barrier, n_dp - 1 + n_t - 1)

    own_rows = rows_of(t * n_dp + d, rows)
    order = (4, 3, 5, 2, 6, 1, 7)
    for k in order:
        send(grad_out.at[:, cols_of(lax.rem(d + k, n_dp))], gcols.at[own_rows],
             a2a_s.at[0, k], a2a_r.at[0, k], dp_peer(k))
    gcols[own_rows, :] = grad_out[:, cols_of(d)]
    floated = tokens[...].astype(jnp.float32)
    inv_rms[...] = lax.rsqrt(jnp.mean(floated * floated, axis=-1, keepdims=True) + epsilon)
    for i in range(n_dp):
        s = pl.ds(i * columns, columns)
        normed[:, s] = (
            tokens[:, s].astype(jnp.float32) * inv_rms[...] * gain_row[:, s].astype(jnp.float32)
        ).astype(jnp.bfloat16)
    for k in order:
        send(normed.at[:, cols_of(lax.rem(d + k, n_dp))], ncols.at[own_rows],
             a2a_s.at[1, k], a2a_r.at[1, k], dp_peer(k))
    ncols[own_rows, :] = normed[:, cols_of(d)]

    own_block = rows_of(t, block)
    y_block = rows_of((1 - y) * 2 + c, block)
    core_block = rows_of(y * 2 + 1 - c, block)
    far_block = rows_of((1 - y) * 2 + 1 - c, block)

    def spread(a, buf):
        for k in order:
            arrived(buf.at[rows_of(t * n_dp + lax.rem(d - k + n_dp, n_dp), rows)],
                    a2a_s.at[a, k], a2a_r.at[a, k])
        send(buf.at[own_block], buf.at[own_block], tens_s.at[a, 0], tens_r.at[a, 0], y_peer)
        send(buf.at[own_block], buf.at[own_block], tens_s.at[a, 1], tens_r.at[a, 1], core_peer)

    def spread_far(a, buf):
        arrived(buf.at[y_block], tens_s.at[a, 0], tens_r.at[a, 0])
        send(buf.at[y_block], buf.at[y_block], tens_s.at[a, 2], tens_r.at[a, 2], core_peer)

    def spread_wait(a, buf):
        arrived(buf.at[core_block], tens_s.at[a, 1], tens_r.at[a, 1])
        arrived(buf.at[far_block], tens_s.at[a, 2], tens_r.at[a, 2])

    def product(a, buf, weight, i):
        prod = lax.dot_general(
            weight[...], buf[rows_of(i, block), :], (((1,), (1,)), ((), ())),
            preferred_element_type=jnp.float32,
        ).astype(jnp.bfloat16)
        part[a, i, 0] = prod[:, :chunk]
        part[a, i, 1] = prod[:, chunk:]

    def to_x(a, i):
        send(part.at[a, i, 1 - x], recvx.at[a, i], x_s.at[a, i], x_r.at[a, i], x_peer)

    def products(a, buf, weight):
        for i in range(n_z):
            product(a, buf, weight, i)
            to_x(a, i)

    def x_sum(a, i):
        return part[a, i, x].astype(jnp.float32) + recvx[a, i].astype(jnp.float32)

    def to_z(a):
        for k in (2, 3, 1):
            i = lax.rem(z + k, n_z)
            arrived(recvx.at[a, i], x_s.at[a, i], x_r.at[a, i])
            sumz[a, k - 1] = x_sum(a, i).astype(jnp.bfloat16)
            send(sumz.at[a, k - 1], recvz.at[a, k - 1], z_s.at[a, k - 1], z_r.at[a, k - 1],
                 z_peer(k))

    def z_wait(a):
        arrived(recvx.at[a, z], x_s.at[a, z], x_r.at[a, z])
        for k in (1, 2, 3):
            arrived(recvz.at[a, k - 1], z_s.at[a, k - 1], z_r.at[a, k - 1])

    def z_sum(a, s):
        total = part[a, z, x, s, :].astype(jnp.float32) + recvx[a, z, s, :].astype(jnp.float32)
        for k in range(3):
            total = total + recvz[a, k, s, :].astype(jnp.float32)
        return total

    spread(0, gcols)
    spread_far(0, gcols)
    spread_wait(0, gcols)
    products(0, gcols, down)
    spread(1, ncols)
    to_z(0)
    spread_far(1, ncols)
    spread_wait(1, ncols)
    products(1, ncols, up)
    to_z(1)
    z_wait(0)
    z_wait(1)

    own_lanes = lanes_of(d)
    whole = pl.ds(0, hidden)
    lifted = jnp.maximum(z_sum(1, whole), 0.0)
    gp[:, own_lanes] = (z_sum(0, whole) * (2.0 * lifted)).astype(jnp.bfloat16)
    hid[:, own_lanes] = (lifted * lifted).astype(jnp.bfloat16)

    def share(a, buf):
        for k in (2, 1, 3):
            send(buf.at[:, own_lanes], buf.at[:, own_lanes], gz_s.at[a, k], gz_r.at[a, k],
                 z_peer(k))
        send(buf.at[:, own_lanes], buf.at[:, own_lanes], gx_s.at[a, 0], gx_r.at[a, 0], x_peer)

    def z_lanes(k, side):
        return lanes_of(lax.rem(z - k + n_z, n_z) * 2 + side)

    def share_far(a, buf):
        for k in (1, 3, 2):
            s = z_lanes(k, x)
            arrived(buf.at[:, s], gz_s.at[a, k], gz_r.at[a, k])
            send(buf.at[:, s], buf.at[:, s], gx_s.at[a, k], gx_r.at[a, k], x_peer)

    def share_wait(a, buf):
        for k in range(n_z):
            arrived(buf.at[:, z_lanes(k, 1 - x)], gx_s.at[a, k], gx_r.at[a, k])

    share(0, gp)
    share(1, hid)
    share_far(0, gp)
    share_wait(0, gp)

    def input_part(i):
        return lax.dot_general(
            gp[:, pl.ds(pl.multiple_of(i * block, 128), block)], up[...],
            (((0,), (0,)), ((), ())), preferred_element_type=jnp.float32,
        )

    for h in range(2):
        q = 1 - y if h == 0 else y
        esend[h] = input_part(q * 2 + 1 - c).astype(jnp.bfloat16)
        send(esend.at[h], ecore.at[h], e_s.at[h], e_r.at[h], core_peer)
    gnf[...] = input_part((1 - y) * 2 + c)
    arrived(ecore.at[0], e_s.at[0], e_r.at[0])
    ysend[...] = (gnf[...] + ecore[0].astype(jnp.float32)).astype(jnp.bfloat16)
    send(ysend, ey, e_s.at[2], e_r.at[2], y_peer)
    gnf[...] = input_part(t)
    arrived(ecore.at[1], e_s.at[1], e_r.at[1])
    gnf[...] = gnf[...] + ecore[1].astype(jnp.float32)
    share_far(1, hid)
    arrived(ey, e_s.at[2], e_r.at[2])
    gnf[...] = gnf[...] + ey[...].astype(jnp.float32)
    gnb[...] = gnf[...].astype(jnp.bfloat16)
    for k in order:
        send(gnb.at[rows_of(lax.rem(d + k, n_dp), rows)], gnrows.at[:, cols_of(d)],
             back_s.at[k], back_r.at[k], dp_peer(k))
    gnrows[:, cols_of(d)] = gnb[rows_of(d, rows), :]

    total = jnp.zeros((8, columns), jnp.float32)
    for i in range(block // 32):
        term = gnf[pl.ds(i * 32, 32), :] * ncols[
            pl.ds(pl.multiple_of(t * block + i * 32, 32), 32), :
        ].astype(jnp.float32)
        total = total + term[0:8] + term[8:16] + term[16:24] + term[24:32]
    gsum[...] = total
    for k in range(1, n_t):
        send(gsum, grecv.at[k - 1], gt_s.at[k - 1], gt_r.at[k - 1], t_peer(k))

    def rows_product(left, right, out):
        half = columns // 3
        for i in range(3):
            s = pl.ds(i * half, half)
            out[:, s] = jnp.dot(
                left[...], right[:, s], preferred_element_type=jnp.float32
            ).astype(jnp.bfloat16)

    rows_product(gp, ncols, out_up)
    for k in range(1, n_t):
        arrived(grecv.at[k - 1], gt_s.at[k - 1], gt_r.at[k - 1])
    total = gsum[...] + grecv[0] + grecv[1] + grecv[2]
    total = jnp.sum(total, axis=0, keepdims=True) / gain_own[...].astype(jnp.float32)
    gshare[d] = jnp.broadcast_to(total, (8, columns))
    for k in order:
        send(gshare.at[d], gshare.at[d], gd_s.at[k], gd_r.at[k], dp_peer(k))
    share_wait(1, hid)
    rows_product(hid, gcols, out_down)

    for k in order:
        arrived(gnrows.at[:, cols_of(lax.rem(d - k + n_dp, n_dp))], back_s.at[k], back_r.at[k])
    inv = inv_rms[...]
    dots = jnp.zeros((rows, 1), jnp.float32)
    for i in range(n_dp):
        s = pl.ds(i * columns, columns)
        dots = dots + jnp.sum(
            gnrows[:, s].astype(jnp.float32) * gain_row[:, s].astype(jnp.float32)
            * (tokens[:, s].astype(jnp.float32) * inv), axis=-1, keepdims=True)
    mean_term = dots / tokens.shape[1]
    for i in range(n_dp):
        s = pl.ds(i * columns, columns)
        unit = tokens[:, s].astype(jnp.float32) * inv
        grad_unit = gnrows[:, s].astype(jnp.float32) * gain_row[:, s].astype(jnp.float32)
        out_tokens[:, s] = (inv * (grad_unit - unit * mean_term)).astype(jnp.bfloat16)
    for k in order:
        arrived(gshare.at[lax.rem(d - k + n_dp, n_dp)], gd_s.at[k], gd_r.at[k])
    for i in range(n_dp):
        out_gain[pl.ds(i, 1), :] = gshare[i, 0:1, :]
    for copy in sent:
        copy.wait_send()


def fused(tokens, gain, up_weight, down_weight, grad_out):
    rows, width = tokens.shape
    hidden, columns = up_weight.shape
    n_dp, n_t = width // columns, 4
    block, chunk = n_dp * rows, n_t * rows
    count = n_t * block
    gain_row = gain.reshape(1, width)
    gain_own = lax.dynamic_slice_in_dim(gain_row, lax.axis_index("dp") * columns, columns, 1)
    vmem = pl.BlockSpec(memory_space=pltpu.VMEM)
    bf16, f32 = jnp.bfloat16, jnp.float32
    pairs = [(2, 8), (2, 3), (2, 4), (2, 3), (2, 4), (2, 4), (3,), (8,), (3,), (8,)]
    sems = []
    for shape in pairs:
        sems += [pltpu.SemaphoreType.DMA(shape), pltpu.SemaphoreType.DMA(shape)]
    flops = 10 * count * hidden * columns
    grad_tokens, grad_gain, grad_up, grad_down = pl.pallas_call(
        kernel,
        out_shape=(
            jax.ShapeDtypeStruct((rows, width), bf16),
            jax.ShapeDtypeStruct((n_dp, columns), f32),
            jax.ShapeDtypeStruct((hidden, columns), bf16),
            jax.ShapeDtypeStruct((hidden, columns), bf16),
        ),
        in_specs=[vmem] * 6,
        out_specs=(vmem,) * 4,
        scratch_shapes=[
            pltpu.VMEM((rows, 1), f32),
            pltpu.VMEM((rows, width), bf16),
            pltpu.VMEM((count, columns), bf16),
            pltpu.VMEM((count, columns), bf16),
            pltpu.VMEM((2, 4, 2, hidden, chunk), bf16),
            pltpu.VMEM((2, 4, hidden, chunk), bf16),
            pltpu.VMEM((2, 3, hidden, chunk), bf16),
            pltpu.VMEM((2, 3, hidden, chunk), bf16),
            pltpu.VMEM((hidden, count), bf16),
            pltpu.VMEM((hidden, count), bf16),
            pltpu.VMEM((2, block, columns), bf16),
            pltpu.VMEM((2, block, columns), bf16),
            pltpu.VMEM((block, columns), bf16),
            pltpu.VMEM((block, columns), bf16),
            pltpu.VMEM((block, columns), f32),
            pltpu.VMEM((block, columns), bf16),
            pltpu.VMEM((rows, width), bf16),
            pltpu.VMEM((8, columns), f32),
            pltpu.VMEM((3, 8, columns), f32),
            pltpu.VMEM((n_dp, 8, columns), f32),
            *sems,
        ],
        compiler_params=pltpu.CompilerParams(
            collective_id=0, has_side_effects=True, vmem_limit_bytes=56 * 1024 * 1024
        ),
        cost_estimate=pl.CostEstimate(flops=flops, bytes_accessed=8 * hidden * columns, transcendentals=0),
    )(tokens, gain_row, gain_own, up_weight, down_weight, grad_out)
    return (grad_tokens, grad_gain.reshape(width), grad_up, grad_down)


def solution(mesh):
    n_dp, n_tensor = mesh.shape["dp"], mesh.shape["tensor"]

    def step(tokens, gain, up_weight, down_weight, grad_out):
        hidden, columns = up_weight.shape
        fits = columns % 128 == 0 and hidden % 16 == 0 and tokens.shape[0] % 16 == 0
        if fits and n_tensor == 4 and n_dp == 8:
            return fused(tokens, gain, up_weight, down_weight, grad_out)
        return local(tokens, gain, up_weight, down_weight, grad_out)

    rows = P(("dp", "tensor"), None)
    weights = P("tensor", "dp")
    return jax.shard_map(
        step,
        mesh=mesh,
        in_specs=(rows, P(), weights, weights, rows),
        out_specs=(rows, P(), weights, weights),
        check_vma=False,
    )
```

```python
import functools

import jax
import jax.numpy as jnp
from jax import lax
from jax.experimental import pallas as pl
from jax.experimental.pallas import tpu as pltpu
from jax.sharding import PartitionSpec as P

MESH = pl.DeviceIdType.MESH

epsilon = 1e-05


def local(tokens, gain, up_weight, down_weight, grad_out):
    gain_float = gain.astype(jnp.float32)
    floated = tokens.astype(jnp.float32)
    inv_rms = lax.rsqrt(jnp.mean(floated * floated, axis=-1, keepdims=True) + epsilon)
    unit_rows = floated * inv_rms
    normed = (unit_rows * gain_float).astype(jnp.bfloat16)

    def to_columns(rows):
        part = lax.all_to_all(rows, "dp", split_axis=1, concat_axis=0, tiled=True)
        return lax.all_gather(part, "tensor", axis=0, tiled=True)

    grads_cols = to_columns(grad_out)
    normed_cols = to_columns(normed)
    contract_last = (((1,), (1,)), ((), ()))
    back_part = lax.dot_general(
        grads_cols, down_weight, contract_last, preferred_element_type=jnp.float32
    ).astype(jnp.bfloat16)
    pre_part = lax.dot_general(
        normed_cols, up_weight, contract_last, preferred_element_type=jnp.float32
    ).astype(jnp.bfloat16)
    back_act = lax.psum_scatter(back_part, "dp", scatter_dimension=0, tiled=True)
    pre_act = lax.psum_scatter(pre_part, "dp", scatter_dimension=0, tiled=True)
    lifted = jnp.maximum(pre_act.astype(jnp.float32), 0.0)
    hidden_part = (lifted * lifted).astype(jnp.bfloat16)
    grad_pre_part = (back_act.astype(jnp.float32) * (2.0 * lifted)).astype(jnp.bfloat16)
    grad_pre = lax.all_gather(grad_pre_part, "dp", axis=0, tiled=True)
    hidden_act = lax.all_gather(hidden_part, "dp", axis=0, tiled=True)
    grad_normed_part = jnp.dot(
        grad_pre, up_weight, preferred_element_type=jnp.float32
    ).astype(jnp.bfloat16)
    grad_normed = lax.psum_scatter(grad_normed_part, "tensor", scatter_dimension=0, tiled=True)
    grad_normed = lax.all_to_all(
        grad_normed, "dp", split_axis=0, concat_axis=1, tiled=True
    ).astype(jnp.float32)
    contract_rows = (((0,), (0,)), ((), ()))
    grad_up = lax.dot_general(
        grad_pre, normed_cols, contract_rows, preferred_element_type=jnp.float32
    ).astype(jnp.bfloat16)
    grad_down = lax.dot_general(
        hidden_act, grads_cols, contract_rows, preferred_element_type=jnp.float32
    ).astype(jnp.bfloat16)
    grad_gain = lax.psum(jnp.sum(grad_normed * unit_rows, axis=0), ("dp", "tensor"))
    grad_unit = grad_normed * gain_float
    mean_term = jnp.mean(grad_unit * unit_rows, axis=-1, keepdims=True)
    grad_tokens = (inv_rms * (grad_unit - unit_rows * mean_term)).astype(jnp.bfloat16)
    return (grad_tokens, grad_gain, grad_up, grad_down)


def kernel(
    tokens, gain, up, down, grad_out,
    out_tokens, out_gain, out_up, out_down,
    inv_rms, gain_row, normed, ncols, gcols, part, recvx, sumz, recvz, gp, hid,
    esend, ecore, ysend, ey, gnf, gnb, gnrows, gsum, grecv, gshare,
    a2a_s, a2a_r, tens_s, tens_r, x_s, x_r, z_s, z_r, gz_s, gz_r, gx_s, gx_r,
    e_s, e_r, ey_s, ey_r, back_s, back_r, gt_s, gt_r, gd_s, gd_r,
):
    n_dp, n_t, n_z = 8, 4, 4
    rows, columns = tokens.shape[0], up.shape[1]
    hidden = up.shape[0]
    block = n_dp * rows
    chunk = n_t * rows
    d, t = lax.axis_index("dp"), lax.axis_index("tensor")
    z, x = d // 2, d % 2
    y, c = t // 2, t % 2
    x_peer = (z * 2 + 1 - x, t)
    y_peer = (d, (1 - y) * 2 + c)
    core_peer = (d, y * 2 + 1 - c)

    def dp_peer(k):
        return (lax.rem(d + k, n_dp), t)

    def z_peer(k):
        return (lax.rem(z + k, n_z) * 2 + x, t)

    def t_peer(k):
        return (d, lax.rem(t + k, n_t))

    def send(src, dst, s, r, to):
        copy = pltpu.make_async_remote_copy(
            src_ref=src, dst_ref=dst, send_sem=s, recv_sem=r, device_id=to, device_id_type=MESH
        )
        copy.start()
        sent.append(copy)

    sent = []

    def arrived(dst, s, r):
        pltpu.make_async_remote_copy(
            src_ref=dst, dst_ref=dst, send_sem=s, recv_sem=r, device_id=x_peer, device_id_type=MESH
        ).wait_recv()

    def cols_of(i):
        return pl.ds(pl.multiple_of(i * columns, 128), columns)

    def rows_of(i, size):
        return pl.ds(pl.multiple_of(i * size, 32), size)

    barrier = pltpu.get_barrier_semaphore()
    for k in range(1, n_dp):
        pl.semaphore_signal(barrier, inc=1, device_id=dp_peer(k), device_id_type=MESH)
    for k in range(1, n_t):
        pl.semaphore_signal(barrier, inc=1, device_id=t_peer(k), device_id_type=MESH)
    pl.semaphore_wait(barrier, n_dp - 1 + n_t - 1)

    own_rows = rows_of(t * n_dp + d, rows)
    order = (4, 3, 5, 2, 6, 1, 7)
    for k in order:
        send(grad_out.at[:, cols_of(lax.rem(d + k, n_dp))], gcols.at[own_rows],
             a2a_s.at[0, k], a2a_r.at[0, k], dp_peer(k))
    gcols[own_rows, :] = grad_out[:, cols_of(d)]
    gain_row[...] = gain[...].astype(jnp.float32).reshape(1, tokens.shape[1])
    floated = tokens[...].astype(jnp.float32)
    inv_rms[...] = lax.rsqrt(jnp.mean(floated * floated, axis=-1, keepdims=True) + epsilon)
    for i in range(n_dp):
        s = pl.ds(i * columns, columns)
        normed[:, s] = (
            tokens[:, s].astype(jnp.float32) * inv_rms[...] * gain_row[:, s]
        ).astype(jnp.bfloat16)
    for k in order[:3]:
        send(normed.at[:, cols_of(lax.rem(d + k, n_dp))], ncols.at[own_rows],
             a2a_s.at[1, k], a2a_r.at[1, k], dp_peer(k))
    ncols[own_rows, :] = normed[:, cols_of(d)]

    core_t, y_t, far_t = y * 2 + 1 - c, (1 - y) * 2 + c, (1 - y) * 2 + 1 - c

    def piece(owner, k):
        return rows_of(owner * n_dp + lax.rem(d - k + n_dp, n_dp), rows)

    def spread(a, buf, ks):
        for k in ks:
            p = piece(t, k)
            if k:
                arrived(buf.at[p], a2a_s.at[a, k], a2a_r.at[a, k])
            send(buf.at[p], buf.at[p], tens_s.at[a, 0, k], tens_r.at[a, 0, k], y_peer)
            send(buf.at[p], buf.at[p], tens_s.at[a, 1, k], tens_r.at[a, 1, k], core_peer)

    def spread_far(a, buf):
        for k in (0,) + order:
            p = piece(y_t, k)
            arrived(buf.at[p], tens_s.at[a, 0, k], tens_r.at[a, 0, k])
            send(buf.at[p], buf.at[p], tens_s.at[a, 2, k], tens_r.at[a, 2, k], core_peer)

    def spread_wait(a, buf, which):
        for k in (0,) + order:
            p = piece(core_t if which == 1 else far_t, k)
            arrived(buf.at[p], tens_s.at[a, which, k], tens_r.at[a, which, k])

    def product(a, buf, weight, i):
        prod = lax.dot_general(
            weight[...], buf[rows_of(i, block), :], (((1,), (1,)), ((), ())),
            preferred_element_type=jnp.float32,
        ).astype(jnp.bfloat16)
        part[a, i, 0] = prod[:, :chunk]
        part[a, i, 1] = prod[:, chunk:]

        send(part.at[a, i, 1 - x], recvx.at[a, i], x_s.at[a, i], x_r.at[a, i], x_peer)

    def x_sum(a, i):
        return part[a, i, x].astype(jnp.float32) + recvx[a, i].astype(jnp.float32)

    def to_z(a):
        for k in (2, 3, 1):
            i = lax.rem(z + k, n_z)
            arrived(recvx.at[a, i], x_s.at[a, i], x_r.at[a, i])
            sumz[a, k - 1] = x_sum(a, i).astype(jnp.bfloat16)
            send(sumz.at[a, k - 1], recvz.at[a, k - 1], z_s.at[a, k - 1], z_r.at[a, k - 1],
                 z_peer(k))

    def z_wait(a):
        arrived(recvx.at[a, z], x_s.at[a, z], x_r.at[a, z])
        for k in (1, 2, 3):
            arrived(recvz.at[a, k - 1], z_s.at[a, k - 1], z_r.at[a, k - 1])

    def z_sum(a, s):
        total = part[a, z, x, s, :].astype(jnp.float32) + recvx[a, z, s, :].astype(jnp.float32)
        for k in range(3):
            total = total + recvz[a, k, s, :].astype(jnp.float32)
        return total

    spread(0, gcols, (0,) + order)
    for k in order[3:]:
        send(normed.at[:, cols_of(lax.rem(d + k, n_dp))], ncols.at[own_rows],
             a2a_s.at[1, k], a2a_r.at[1, k], dp_peer(k))
    product(0, gcols, down, t)
    spread_wait(0, gcols, 1)
    product(0, gcols, down, core_t)
    spread(1, ncols, (0,))
    spread_far(0, gcols)
    product(0, gcols, down, y_t)
    spread(1, ncols, order[:3])
    spread_wait(0, gcols, 2)
    product(0, gcols, down, far_t)
    spread(1, ncols, order[3:])
    product(1, ncols, up, t)
    to_z(0)
    spread_far(1, ncols)
    spread_wait(1, ncols, 1)
    product(1, ncols, up, core_t)
    product(1, ncols, up, y_t)
    spread_wait(1, ncols, 2)
    product(1, ncols, up, far_t)
    to_z(1)
    z_wait(0)
    z_wait(1)

    whole = pl.ds(0, hidden)
    lifted = jnp.maximum(z_sum(1, whole), 0.0)
    gp[d] = (z_sum(0, whole) * (2.0 * lifted)).astype(jnp.bfloat16)
    hid[d] = (lifted * lifted).astype(jnp.bfloat16)

    def share(a, buf):
        for k in (2, 1, 3):
            send(buf.at[d], buf.at[d], gz_s.at[a, k], gz_r.at[a, k],
                 z_peer(k))
        send(buf.at[d], buf.at[d], gx_s.at[a, 0], gx_r.at[a, 0], x_peer)

    def z_lanes(k, side):
        return lax.rem(z - k + n_z, n_z) * 2 + side

    def share_far(a, buf):
        for k in (1, 3, 2):
            s = z_lanes(k, x)
            arrived(buf.at[s], gz_s.at[a, k], gz_r.at[a, k])
            send(buf.at[s], buf.at[s], gx_s.at[a, k], gx_r.at[a, k], x_peer)

    def share_wait(a, buf, i):
        k = lax.rem(z - i + n_z, n_z)
        arrived(buf.at[i * 2 + 1 - x], gx_s.at[a, k], gx_r.at[a, k])

    share(0, gp)
    share_far(0, gp)
    share(1, hid)

    def input_part(i):
        return lax.dot_general(
            jnp.concatenate([gp[i * 2], gp[i * 2 + 1]], axis=1), up[...],
            (((0,), (0,)), ((), ())), preferred_element_type=jnp.float32,
        )

    for h in range(2):
        i = far_t if h == 0 else core_t
        share_wait(0, gp, i)
        esend[h] = input_part(i).astype(jnp.bfloat16)
        send(esend.at[h], ecore.at[h], e_s.at[h], e_r.at[h], core_peer)
    share_wait(0, gp, y_t)
    gnf[...] = input_part(y_t)
    arrived(ecore.at[0], e_s.at[0], e_r.at[0])

    def part_rows(k):
        return rows_of(lax.rem(z + k, n_z), 2 * rows)

    parts = (2, 3, 1, 0)
    for k in parts:
        r = part_rows(k)
        ysend[r, :] = (gnf[r, :] + ecore[0, r, :].astype(jnp.float32)).astype(jnp.bfloat16)
        send(ysend.at[r], ey.at[r], ey_s.at[k], ey_r.at[k], y_peer)
    share_wait(0, gp, t)
    gnf[...] = input_part(t)
    arrived(ecore.at[1], e_s.at[1], e_r.at[1])
    for k in parts:
        r = part_rows(k)
        arrived(ey.at[r], ey_s.at[k], ey_r.at[k])
        total = gnf[r, :] + ecore[1, r, :].astype(jnp.float32) + ey[r, :].astype(jnp.float32)
        gnf[r, :] = total
        gnb[r, :] = total.astype(jnp.bfloat16)
        i = lax.rem(z + k, n_z) * 2
        send(gnb.at[rows_of(i + 1 - x, rows)], gnrows.at[:, cols_of(d)],
             back_s.at[k, 0], back_r.at[k, 0], (i + 1 - x, t))
        if k:
            send(gnb.at[rows_of(i + x, rows)], gnrows.at[:, cols_of(d)],
                 back_s.at[k, 1], back_r.at[k, 1], (i + x, t))
    share_far(1, hid)
    gnrows[:, cols_of(d)] = gnb[rows_of(d, rows), :]

    total = jnp.zeros((8, columns), jnp.float32)
    for i in range(block // 32):
        term = gnf[pl.ds(i * 32, 32), :] * ncols[
            pl.ds(pl.multiple_of(t * block + i * 32, 32), 32), :
        ].astype(jnp.float32)
        total = total + term[0:8] + term[8:16] + term[16:24] + term[24:32]
    gsum[...] = total
    for k in range(1, n_t):
        send(gsum, grecv.at[k - 1], gt_s.at[k - 1], gt_r.at[k - 1], t_peer(k))

    def rows_product(left, right, out):
        half = columns // 3
        lanes = jnp.concatenate([left[i] for i in range(n_dp)], axis=1)
        for i in range(3):
            s = pl.ds(i * half, half)
            out[:, s] = jnp.dot(
                lanes, right[:, s], preferred_element_type=jnp.float32
            ).astype(jnp.bfloat16)

    rows_product(gp, ncols, out_up)
    for k in range(1, n_t):
        arrived(grecv.at[k - 1], gt_s.at[k - 1], gt_r.at[k - 1])
    total = gsum[...] + grecv[0] + grecv[1] + grecv[2]
    total = jnp.sum(total, axis=0, keepdims=True) / gain_row[:, cols_of(d)]
    gshare[d] = jnp.broadcast_to(total, (8, columns))
    for k in order:
        send(gshare.at[d], gshare.at[d], gd_s.at[k], gd_r.at[k], dp_peer(k))
    for i in range(n_z):
        share_wait(1, hid, i)
    rows_product(hid, gcols, out_down)

    for k in parts:
        i = lax.rem(z - k + n_z, n_z) * 2
        arrived(gnrows.at[:, cols_of(i + 1 - x)], back_s.at[k, 0], back_r.at[k, 0])
        if k:
            arrived(gnrows.at[:, cols_of(i + x)], back_s.at[k, 1], back_r.at[k, 1])
    inv = inv_rms[...]
    dots = jnp.zeros((rows, 1), jnp.float32)
    for i in range(n_dp):
        s = pl.ds(i * columns, columns)
        dots = dots + jnp.sum(
            gnrows[:, s].astype(jnp.float32) * gain_row[:, s]
            * (tokens[:, s].astype(jnp.float32) * inv), axis=-1, keepdims=True)
    mean_term = dots / tokens.shape[1]
    for i in range(n_dp):
        s = pl.ds(i * columns, columns)
        unit = tokens[:, s].astype(jnp.float32) * inv
        grad_unit = gnrows[:, s].astype(jnp.float32) * gain_row[:, s]
        out_tokens[:, s] = (inv * (grad_unit - unit * mean_term)).astype(jnp.bfloat16)
    for k in order:
        arrived(gshare.at[lax.rem(d - k + n_dp, n_dp)], gd_s.at[k], gd_r.at[k])
    for i in range(n_dp):
        out_gain[pl.ds(i * columns, columns)] = gshare[i, 0:1, :].reshape(columns)
    for copy in sent:
        copy.wait_send()


def fused(tokens, gain, up_weight, down_weight, grad_out):
    rows, width = tokens.shape
    hidden, columns = up_weight.shape
    n_dp, n_t = width // columns, 4
    block, chunk = n_dp * rows, n_t * rows
    count = n_t * block
    vmem = pl.BlockSpec(memory_space=pltpu.VMEM)
    bf16, f32 = jnp.bfloat16, jnp.float32
    pairs = [(2, 8), (2, 3, 8), (2, 4), (2, 3), (2, 4), (2, 4), (2,), (4,), (4, 2), (3,), (8,)]
    sems = []
    for shape in pairs:
        sems += [pltpu.SemaphoreType.DMA(shape), pltpu.SemaphoreType.DMA(shape)]
    flops = 10 * count * hidden * columns
    grad_tokens, grad_gain, grad_up, grad_down = pl.pallas_call(
        kernel,
        out_shape=(
            jax.ShapeDtypeStruct((rows, width), bf16),
            jax.ShapeDtypeStruct((width,), f32),
            jax.ShapeDtypeStruct((hidden, columns), bf16),
            jax.ShapeDtypeStruct((hidden, columns), bf16),
        ),
        in_specs=[vmem] * 5,
        out_specs=(vmem,) * 4,
        scratch_shapes=[
            pltpu.VMEM((rows, 1), f32),
            pltpu.VMEM((1, width), f32),
            pltpu.VMEM((rows, width), bf16),
            pltpu.VMEM((count, columns), bf16),
            pltpu.VMEM((count, columns), bf16),
            pltpu.VMEM((2, 4, 2, hidden, chunk), bf16),
            pltpu.VMEM((2, 4, hidden, chunk), bf16),
            pltpu.VMEM((2, 3, hidden, chunk), bf16),
            pltpu.VMEM((2, 3, hidden, chunk), bf16),
            pltpu.VMEM((n_dp, hidden, chunk), bf16),
            pltpu.VMEM((n_dp, hidden, chunk), bf16),
            pltpu.VMEM((2, block, columns), bf16),
            pltpu.VMEM((2, block, columns), bf16),
            pltpu.VMEM((block, columns), bf16),
            pltpu.VMEM((block, columns), bf16),
            pltpu.VMEM((block, columns), f32),
            pltpu.VMEM((block, columns), bf16),
            pltpu.VMEM((rows, width), bf16),
            pltpu.VMEM((8, columns), f32),
            pltpu.VMEM((3, 8, columns), f32),
            pltpu.VMEM((n_dp, 8, columns), f32),
            *sems,
        ],
        compiler_params=pltpu.CompilerParams(
            collective_id=0, has_side_effects=True, vmem_limit_bytes=56 * 1024 * 1024
        ),
        cost_estimate=pl.CostEstimate(flops=flops, bytes_accessed=8 * hidden * columns, transcendentals=0),
    )(tokens, gain, up_weight, down_weight, grad_out)
    return (grad_tokens, grad_gain, grad_up, grad_down)


def solution(mesh):
    n_dp, n_tensor = mesh.shape["dp"], mesh.shape["tensor"]

    def step(tokens, gain, up_weight, down_weight, grad_out):
        hidden, columns = up_weight.shape
        fits = columns % 128 == 0 and hidden % 16 == 0 and tokens.shape[0] % 16 == 0
        if fits and n_tensor == 4 and n_dp == 8:
            return fused(tokens, gain, up_weight, down_weight, grad_out)
        return local(tokens, gain, up_weight, down_weight, grad_out)

    rows = P(("dp", "tensor"), None)
    weights = P("tensor", "dp")
    return jax.shard_map(
        step,
        mesh=mesh,
        in_specs=(rows, P(), weights, weights, rows),
        out_specs=(rows, P(), weights, weights),
        check_vma=False,
    )
```

```python
import functools

import jax
import jax.numpy as jnp
from jax import lax
from jax.experimental import pallas as pl
from jax.experimental.pallas import tpu as pltpu
from jax.sharding import PartitionSpec as P

MESH = pl.DeviceIdType.MESH

epsilon = 1e-05


def local(tokens, gain, up_weight, down_weight, grad_out):
    gain_float = gain.astype(jnp.float32)
    floated = tokens.astype(jnp.float32)
    inv_rms = lax.rsqrt(jnp.mean(floated * floated, axis=-1, keepdims=True) + epsilon)
    unit_rows = floated * inv_rms
    normed = (unit_rows * gain_float).astype(jnp.bfloat16)

    def to_columns(rows):
        part = lax.all_to_all(rows, "dp", split_axis=1, concat_axis=0, tiled=True)
        return lax.all_gather(part, "tensor", axis=0, tiled=True)

    grads_cols = to_columns(grad_out)
    normed_cols = to_columns(normed)
    contract_last = (((1,), (1,)), ((), ()))
    back_part = lax.dot_general(
        grads_cols, down_weight, contract_last, preferred_element_type=jnp.float32
    ).astype(jnp.bfloat16)
    pre_part = lax.dot_general(
        normed_cols, up_weight, contract_last, preferred_element_type=jnp.float32
    ).astype(jnp.bfloat16)
    back_act = lax.psum_scatter(back_part, "dp", scatter_dimension=0, tiled=True)
    pre_act = lax.psum_scatter(pre_part, "dp", scatter_dimension=0, tiled=True)
    lifted = jnp.maximum(pre_act.astype(jnp.float32), 0.0)
    hidden_part = (lifted * lifted).astype(jnp.bfloat16)
    grad_pre_part = (back_act.astype(jnp.float32) * (2.0 * lifted)).astype(jnp.bfloat16)
    grad_pre = lax.all_gather(grad_pre_part, "dp", axis=0, tiled=True)
    hidden_act = lax.all_gather(hidden_part, "dp", axis=0, tiled=True)
    grad_normed_part = jnp.dot(
        grad_pre, up_weight, preferred_element_type=jnp.float32
    ).astype(jnp.bfloat16)
    grad_normed = lax.psum_scatter(grad_normed_part, "tensor", scatter_dimension=0, tiled=True)
    grad_normed = lax.all_to_all(
        grad_normed, "dp", split_axis=0, concat_axis=1, tiled=True
    ).astype(jnp.float32)
    contract_rows = (((0,), (0,)), ((), ()))
    grad_up = lax.dot_general(
        grad_pre, normed_cols, contract_rows, preferred_element_type=jnp.float32
    ).astype(jnp.bfloat16)
    grad_down = lax.dot_general(
        hidden_act, grads_cols, contract_rows, preferred_element_type=jnp.float32
    ).astype(jnp.bfloat16)
    grad_gain = lax.psum(jnp.sum(grad_normed * unit_rows, axis=0), ("dp", "tensor"))
    grad_unit = grad_normed * gain_float
    mean_term = jnp.mean(grad_unit * unit_rows, axis=-1, keepdims=True)
    grad_tokens = (inv_rms * (grad_unit - unit_rows * mean_term)).astype(jnp.bfloat16)
    return (grad_tokens, grad_gain, grad_up, grad_down)


def kernel(
    tokens, gain, up, down, grad_out,
    out_tokens, out_gain, out_up, out_down,
    inv_rms, gain_row, normed, ncols, gcols, part, recvx, sumz, recvz, gp, hid,
    esend, ecore, ysend, ey, gnf, gnb, gnrows, gsum, grecv, gshare,
    a2a_s, a2a_r, tens_s, tens_r, x_s, x_r, z_s, z_r, gz_s, gz_r, gx_s, gx_r,
    e_s, e_r, ey_s, ey_r, back_s, back_r, gt_s, gt_r, gd_s, gd_r,
):
    n_dp, n_t, n_z = 8, 4, 4
    rows, columns = tokens.shape[0], up.shape[1]
    hidden = up.shape[0]
    block = n_dp * rows
    chunk = n_t * rows
    d, t = lax.axis_index("dp"), lax.axis_index("tensor")
    z, x = d // 2, d % 2
    y, c = t // 2, t % 2
    x_peer = (z * 2 + 1 - x, t)
    y_peer = (d, (1 - y) * 2 + c)
    core_peer = (d, y * 2 + 1 - c)

    def dp_peer(k):
        return (lax.rem(d + k, n_dp), t)

    def z_peer(k):
        return (lax.rem(z + k, n_z) * 2 + x, t)

    def t_peer(k):
        return (d, lax.rem(t + k, n_t))

    def send(src, dst, s, r, to):
        copy = pltpu.make_async_remote_copy(
            src_ref=src, dst_ref=dst, send_sem=s, recv_sem=r, device_id=to, device_id_type=MESH
        )
        copy.start()
        sent.append(copy)

    sent = []

    def arrived(dst, s, r):
        pltpu.make_async_remote_copy(
            src_ref=dst, dst_ref=dst, send_sem=s, recv_sem=r, device_id=x_peer, device_id_type=MESH
        ).wait_recv()

    def cols_of(i):
        return pl.ds(pl.multiple_of(i * columns, 128), columns)

    def rows_of(i, size):
        return pl.ds(pl.multiple_of(i * size, 32), size)

    barrier = pltpu.get_barrier_semaphore()
    for k in range(1, n_dp):
        pl.semaphore_signal(barrier, inc=1, device_id=dp_peer(k), device_id_type=MESH)
    for k in range(1, n_t):
        pl.semaphore_signal(barrier, inc=1, device_id=t_peer(k), device_id_type=MESH)
    pl.semaphore_wait(barrier, n_dp - 1 + n_t - 1)

    own_rows = rows_of(t * n_dp + d, rows)
    order = (4, 3, 5, 2, 6, 1, 7)
    for k in order:
        send(grad_out.at[:, cols_of(lax.rem(d + k, n_dp))], gcols.at[own_rows],
             a2a_s.at[0, k], a2a_r.at[0, k], dp_peer(k))
    gcols[own_rows, :] = grad_out[:, cols_of(d)]
    gain_row[...] = gain[...].astype(jnp.float32).reshape(1, tokens.shape[1])
    floated = tokens[...].astype(jnp.float32)
    inv_rms[...] = lax.rsqrt(jnp.mean(floated * floated, axis=-1, keepdims=True) + epsilon)
    for i in range(n_dp):
        s = pl.ds(i * columns, columns)
        normed[:, s] = (
            tokens[:, s].astype(jnp.float32) * inv_rms[...] * gain_row[:, s]
        ).astype(jnp.bfloat16)
    for k in order[:3]:
        send(normed.at[:, cols_of(lax.rem(d + k, n_dp))], ncols.at[own_rows],
             a2a_s.at[1, k], a2a_r.at[1, k], dp_peer(k))
    ncols[own_rows, :] = normed[:, cols_of(d)]

    core_t, y_t, far_t = y * 2 + 1 - c, (1 - y) * 2 + c, (1 - y) * 2 + 1 - c

    def piece(owner, k):
        return rows_of(owner * n_dp + lax.rem(d - k + n_dp, n_dp), rows)

    def spread(a, buf, ks):
        for k in ks:
            p = piece(t, k)
            if k:
                arrived(buf.at[p], a2a_s.at[a, k], a2a_r.at[a, k])
            send(buf.at[p], buf.at[p], tens_s.at[a, 0, k], tens_r.at[a, 0, k], y_peer)
            send(buf.at[p], buf.at[p], tens_s.at[a, 1, k], tens_r.at[a, 1, k], core_peer)

    def spread_far(a, buf):
        for k in (0,) + order:
            p = piece(y_t, k)
            arrived(buf.at[p], tens_s.at[a, 0, k], tens_r.at[a, 0, k])
            send(buf.at[p], buf.at[p], tens_s.at[a, 2, k], tens_r.at[a, 2, k], core_peer)

    def spread_wait(a, buf, which):
        for k in (0,) + order:
            p = piece(core_t if which == 1 else far_t, k)
            arrived(buf.at[p], tens_s.at[a, which, k], tens_r.at[a, which, k])

    def product(a, buf, weight, i):
        prod = lax.dot_general(
            weight[...], buf[rows_of(i, block), :], (((1,), (1,)), ((), ())),
            preferred_element_type=jnp.float32,
        ).astype(jnp.bfloat16)
        part[a, i, 0] = prod[:, :chunk]
        part[a, i, 1] = prod[:, chunk:]

        send(part.at[a, i, 1 - x], recvx.at[a, i], x_s.at[a, i], x_r.at[a, i], x_peer)

    def x_sum(a, i):
        return part[a, i, x].astype(jnp.float32) + recvx[a, i].astype(jnp.float32)

    def to_z(a, i):
        k = lax.rem(i - z + n_z, n_z)

        @pl.when(k != 0)
        def _():
            arrived(recvx.at[a, i], x_s.at[a, i], x_r.at[a, i])
            sumz[a, k - 1] = x_sum(a, i).astype(jnp.bfloat16)
            z_copy(a, k).start()

    def z_copy(a, k):
        return pltpu.make_async_remote_copy(
            src_ref=sumz.at[a, k - 1], dst_ref=recvz.at[a, k - 1], send_sem=z_s.at[a, k - 1],
            recv_sem=z_r.at[a, k - 1], device_id=z_peer(k), device_id_type=MESH,
        )

    def z_wait(a):
        arrived(recvx.at[a, z], x_s.at[a, z], x_r.at[a, z])
        for k in (1, 2, 3):
            arrived(recvz.at[a, k - 1], z_s.at[a, k - 1], z_r.at[a, k - 1])

    def z_sum(a, s):
        total = part[a, z, x, s, :].astype(jnp.float32) + recvx[a, z, s, :].astype(jnp.float32)
        for k in range(3):
            total = total + recvz[a, k, s, :].astype(jnp.float32)
        return total

    spread(0, gcols, (0,) + order)
    for k in order[3:]:
        send(normed.at[:, cols_of(lax.rem(d + k, n_dp))], ncols.at[own_rows],
             a2a_s.at[1, k], a2a_r.at[1, k], dp_peer(k))
    product(0, gcols, down, t)
    spread_wait(0, gcols, 1)
    product(0, gcols, down, core_t)
    spread(1, ncols, (0,))
    spread_far(0, gcols)
    product(0, gcols, down, y_t)
    spread(1, ncols, order[:3])
    spread_wait(0, gcols, 2)
    product(0, gcols, down, far_t)
    spread(1, ncols, order[3:])
    product(1, ncols, up, t)
    for i in (t, core_t, y_t, far_t):
        to_z(0, i)
    spread_wait(1, ncols, 1)
    product(1, ncols, up, core_t)
    to_z(1, t)
    to_z(1, core_t)
    spread_far(1, ncols)
    product(1, ncols, up, y_t)
    spread_wait(1, ncols, 2)
    product(1, ncols, up, far_t)
    to_z(1, y_t)
    to_z(1, far_t)
    z_wait(0)
    z_wait(1)

    whole = pl.ds(0, hidden)
    lifted = jnp.maximum(z_sum(1, whole), 0.0)
    gp[d] = (z_sum(0, whole) * (2.0 * lifted)).astype(jnp.bfloat16)
    hid[d] = (lifted * lifted).astype(jnp.bfloat16)

    def share(a, buf):
        for k in (2, 1, 3):
            send(buf.at[d], buf.at[d], gz_s.at[a, k], gz_r.at[a, k],
                 z_peer(k))
        send(buf.at[d], buf.at[d], gx_s.at[a, 0], gx_r.at[a, 0], x_peer)

    def z_lanes(k, side):
        return lax.rem(z - k + n_z, n_z) * 2 + side

    def share_far(a, buf):
        for k in (1, 3, 2):
            s = z_lanes(k, x)
            arrived(buf.at[s], gz_s.at[a, k], gz_r.at[a, k])
            send(buf.at[s], buf.at[s], gx_s.at[a, k], gx_r.at[a, k], x_peer)

    def share_wait(a, buf, i):
        k = lax.rem(z - i + n_z, n_z)
        arrived(buf.at[i * 2 + 1 - x], gx_s.at[a, k], gx_r.at[a, k])

    share(0, gp)
    share_far(0, gp)
    share(1, hid)

    def input_part(i):
        return lax.dot_general(
            jnp.concatenate([gp[i * 2], gp[i * 2 + 1]], axis=1), up[...],
            (((0,), (0,)), ((), ())), preferred_element_type=jnp.float32,
        )

    for h in range(2):
        i = far_t if h == 0 else core_t
        share_wait(0, gp, i)
        esend[h] = input_part(i).astype(jnp.bfloat16)
        send(esend.at[h], ecore.at[h], e_s.at[h], e_r.at[h], core_peer)
    share_wait(0, gp, y_t)
    gnf[...] = input_part(y_t)
    arrived(ecore.at[0], e_s.at[0], e_r.at[0])

    def part_rows(k):
        return rows_of(lax.rem(z + k, n_z), 2 * rows)

    parts = (2, 3, 1, 0)
    for k in parts:
        r = part_rows(k)
        ysend[r, :] = (gnf[r, :] + ecore[0, r, :].astype(jnp.float32)).astype(jnp.bfloat16)
        send(ysend.at[r], ey.at[r], ey_s.at[k], ey_r.at[k], y_peer)
    share_far(1, hid)
    share_wait(0, gp, t)
    gnf[...] = input_part(t)
    arrived(ecore.at[1], e_s.at[1], e_r.at[1])
    for k in parts:
        r = part_rows(k)
        arrived(ey.at[r], ey_s.at[k], ey_r.at[k])
        total = gnf[r, :] + ecore[1, r, :].astype(jnp.float32) + ey[r, :].astype(jnp.float32)
        gnf[r, :] = total
        gnb[r, :] = total.astype(jnp.bfloat16)
        i = lax.rem(z + k, n_z) * 2
        send(gnb.at[rows_of(i + 1 - x, rows)], gnrows.at[:, cols_of(d)],
             back_s.at[k, 0], back_r.at[k, 0], (i + 1 - x, t))
        if k:
            send(gnb.at[rows_of(i + x, rows)], gnrows.at[:, cols_of(d)],
                 back_s.at[k, 1], back_r.at[k, 1], (i + x, t))
    gnrows[:, cols_of(d)] = gnb[rows_of(d, rows), :]

    total = jnp.zeros((8, columns), jnp.float32)
    for i in range(block // 32):
        term = gnf[pl.ds(i * 32, 32), :] * ncols[
            pl.ds(pl.multiple_of(t * block + i * 32, 32), 32), :
        ].astype(jnp.float32)
        total = total + term[0:8] + term[8:16] + term[16:24] + term[24:32]
    gsum[...] = total
    for k in range(1, n_t):
        send(gsum, grecv.at[k - 1], gt_s.at[k - 1], gt_r.at[k - 1], t_peer(k))

    def rows_product(left, right, out):
        half = columns // 3
        lanes = jnp.concatenate([left[i] for i in range(n_dp)], axis=1)
        for i in range(3):
            s = pl.ds(i * half, half)
            out[:, s] = jnp.dot(
                lanes, right[:, s], preferred_element_type=jnp.float32
            ).astype(jnp.bfloat16)

    rows_product(gp, ncols, out_up)
    for k in range(1, n_t):
        arrived(grecv.at[k - 1], gt_s.at[k - 1], gt_r.at[k - 1])
    total = gsum[...] + grecv[0] + grecv[1] + grecv[2]
    total = jnp.sum(total, axis=0, keepdims=True) / gain_row[:, cols_of(d)]
    gshare[d] = jnp.broadcast_to(total, (8, columns))
    for k in order:
        send(gshare.at[d], gshare.at[d], gd_s.at[k], gd_r.at[k], dp_peer(k))
    for i in range(n_z):
        share_wait(1, hid, i)
    rows_product(hid, gcols, out_down)

    for k in parts:
        i = lax.rem(z - k + n_z, n_z) * 2
        arrived(gnrows.at[:, cols_of(i + 1 - x)], back_s.at[k, 0], back_r.at[k, 0])
        if k:
            arrived(gnrows.at[:, cols_of(i + x)], back_s.at[k, 1], back_r.at[k, 1])
    inv = inv_rms[...]
    dots = jnp.zeros((rows, 1), jnp.float32)
    for i in range(n_dp):
        s = pl.ds(i * columns, columns)
        dots = dots + jnp.sum(
            gnrows[:, s].astype(jnp.float32) * gain_row[:, s]
            * (tokens[:, s].astype(jnp.float32) * inv), axis=-1, keepdims=True)
    mean_term = dots / tokens.shape[1]
    for i in range(n_dp):
        s = pl.ds(i * columns, columns)
        unit = tokens[:, s].astype(jnp.float32) * inv
        grad_unit = gnrows[:, s].astype(jnp.float32) * gain_row[:, s]
        out_tokens[:, s] = (inv * (grad_unit - unit * mean_term)).astype(jnp.bfloat16)
    for k in order:
        arrived(gshare.at[lax.rem(d - k + n_dp, n_dp)], gd_s.at[k], gd_r.at[k])
    for i in range(n_dp):
        out_gain[pl.ds(i * columns, columns)] = gshare[i, 0:1, :].reshape(columns)
    for a in range(2):
        for k in (1, 2, 3):
            z_copy(a, k).wait_send()
    for copy in sent:
        copy.wait_send()


def fused(tokens, gain, up_weight, down_weight, grad_out):
    rows, width = tokens.shape
    hidden, columns = up_weight.shape
    n_dp, n_t = width // columns, 4
    block, chunk = n_dp * rows, n_t * rows
    count = n_t * block
    vmem = pl.BlockSpec(memory_space=pltpu.VMEM)
    bf16, f32 = jnp.bfloat16, jnp.float32
    pairs = [(2, 8), (2, 3, 8), (2, 4), (2, 3), (2, 4), (2, 4), (2,), (4,), (4, 2), (3,), (8,)]
    sems = []
    for shape in pairs:
        sems += [pltpu.SemaphoreType.DMA(shape), pltpu.SemaphoreType.DMA(shape)]
    flops = 10 * count * hidden * columns
    grad_tokens, grad_gain, grad_up, grad_down = pl.pallas_call(
        kernel,
        out_shape=(
            jax.ShapeDtypeStruct((rows, width), bf16),
            jax.ShapeDtypeStruct((width,), f32),
            jax.ShapeDtypeStruct((hidden, columns), bf16),
            jax.ShapeDtypeStruct((hidden, columns), bf16),
        ),
        in_specs=[vmem] * 5,
        out_specs=(vmem,) * 4,
        scratch_shapes=[
            pltpu.VMEM((rows, 1), f32),
            pltpu.VMEM((1, width), f32),
            pltpu.VMEM((rows, width), bf16),
            pltpu.VMEM((count, columns), bf16),
            pltpu.VMEM((count, columns), bf16),
            pltpu.VMEM((2, 4, 2, hidden, chunk), bf16),
            pltpu.VMEM((2, 4, hidden, chunk), bf16),
            pltpu.VMEM((2, 3, hidden, chunk), bf16),
            pltpu.VMEM((2, 3, hidden, chunk), bf16),
            pltpu.VMEM((n_dp, hidden, chunk), bf16),
            pltpu.VMEM((n_dp, hidden, chunk), bf16),
            pltpu.VMEM((2, block, columns), bf16),
            pltpu.VMEM((2, block, columns), bf16),
            pltpu.VMEM((block, columns), bf16),
            pltpu.VMEM((block, columns), bf16),
            pltpu.VMEM((block, columns), f32),
            pltpu.VMEM((block, columns), bf16),
            pltpu.VMEM((rows, width), bf16),
            pltpu.VMEM((8, columns), f32),
            pltpu.VMEM((3, 8, columns), f32),
            pltpu.VMEM((n_dp, 8, columns), f32),
            *sems,
        ],
        compiler_params=pltpu.CompilerParams(
            collective_id=0, has_side_effects=True, vmem_limit_bytes=56 * 1024 * 1024
        ),
        cost_estimate=pl.CostEstimate(flops=flops, bytes_accessed=8 * hidden * columns, transcendentals=0),
    )(tokens, gain, up_weight, down_weight, grad_out)
    return (grad_tokens, grad_gain, grad_up, grad_down)


def solution(mesh):
    n_dp, n_tensor = mesh.shape["dp"], mesh.shape["tensor"]

    def step(tokens, gain, up_weight, down_weight, grad_out):
        hidden, columns = up_weight.shape
        fits = columns % 128 == 0 and hidden % 16 == 0 and tokens.shape[0] % 16 == 0
        if fits and n_tensor == 4 and n_dp == 8:
            return fused(tokens, gain, up_weight, down_weight, grad_out)
        return local(tokens, gain, up_weight, down_weight, grad_out)

    rows = P(("dp", "tensor"), None)
    weights = P("tensor", "dp")
    return jax.shard_map(
        step,
        mesh=mesh,
        in_specs=(rows, P(), weights, weights, rows),
        out_specs=(rows, P(), weights, weights),
        check_vma=False,
    )
```
